32 devices in a mesh: row: 4 (over z), col: 8 (over y, x, core).
Axes of the slice: x: 2, y: 2, z: 4, core: 2. Of those that a mesh axis runs over, the one named last changes fastest.
Arguments:
- flow_state: bfloat16 [8192, 256], P(('col', 'row')), may hold values from -6 to 6
- link_state: bfloat16 [4096, 256], P(('row', 'col')), may hold values from -6 to 6
- incidence: bfloat16 [4, 8, 24, 128, 128], P('row', 'col'), may hold values from -0.29882812 to 0.29882812
- tile_flow: int32 [4, 8, 24], P('row', 'col'), may hold values from 0 to 7
- tile_link: int32 [4, 8, 24], P('row', 'col'), may hold values from 0 to 7
- tile_live: int32 [4, 8, 24], P('row', 'col'), may hold values from 0 to 1, as said below
- link_gain: float32 [256], replicated, may hold values from 0.5 to 2
- link_agg_weight: bfloat16 [256, 256], replicated, may hold values from -0.375 to 0.375
- link_self_weight: bfloat16 [256, 256], replicated, may hold values from -0.375 to 0.375
- link_out_weight: bfloat16 [256, 256], replicated, may hold values from -0.375 to 0.375
- flow_gain: float32 [256], replicated, may hold values from 0.5 to 2
- flow_agg_weight: bfloat16 [256, 256], replicated, may hold values from -0.375 to 0.375
- flow_self_weight: bfloat16 [256, 256], replicated, may hold values from -0.375 to 0.375
- flow_out_weight: bfloat16 [256, 256], replicated, may hold values from -0.375 to 0.375
Outputs:
- link_next: bfloat16 [4096, 256], P(('row', 'col'))
- flow_next: bfloat16 [8192, 256], P(('col', 'row'))
The draws below stay inside these ranges and needn't reach their ends.
Inputs may be any that keep to these rules, and one draw needn't show every extreme that they name: `tile_live`: in every draw some group pair has all 24 slots live; the number of live slots differs from pair to pair.
All inputs are finite; a program needn't handle non-finite values.
Results may differ from the reference program's by a relative error of at most 0.018.
Values may be sent and summed in bfloat16 or wider, within the bound.
A program may use at most 64 MiB of HBM per device.

```python
import math
import jax
import jax.numpy as jnp
import numpy as np
from jax import lax

H = 256
BS = 128
TMAX = 24
LGROUPS = 4
FGROUPS = 8
FGB = 8
LGB = 8
FLOWS = 8192
LINKS = 4096


def draw_tile_live(key, part):
    key_level, key_pick, key_order = jax.random.split(jax.random.fold_in(key, 7), 3)
    pairs = LGROUPS * FGROUPS
    level = jax.random.randint(key_level, (pairs,), 1, 9)
    filled = jnp.maximum(TMAX * level * level // 64, 1)
    chosen = jax.random.randint(key_pick, (), 0, pairs)
    filled = jnp.where(jnp.arange(pairs) == chosen, TMAX, filled)
    scores = jax.random.randint(key_order, (pairs, TMAX), 0, 2 ** 20) * TMAX + jnp.arange(TMAX)[None, :]
    ranking = jnp.argsort(jnp.argsort(scores, axis=1), axis=1)
    living = (ranking < filled[:, None]).astype(jnp.int32)
    return living.reshape(LGROUPS, FGROUPS, TMAX)


def set_ends(drawn, rng, least, high):
    place = [jax.random.randint(jax.random.fold_in(rng, axis), (), 0, length) for axis, length in enumerate(drawn.shape)]
    widest = drawn.shape.index(max(drawn.shape))
    next_to = place[:widest] + [(place[widest] + 1) % drawn.shape[widest]] + place[widest + 1:]
    return drawn.at[tuple(place)].set(least).at[tuple(next_to)].set(high)


def block_levels(own_key, shape, cuts, least, largest):
    loudness, own = 1.0, jax.random.fold_in(own_key, 6)
    for position, blocks in cuts:
        draws = jnp.exp(jax.random.uniform(jax.random.fold_in(own, position), (blocks,), jnp.float32, least / len(cuts), largest / len(cuts)))
        loudness = loudness * jnp.repeat(draws, shape[position] // blocks).reshape([-1 if axis == position else 1 for axis in range(len(shape))])
    return loudness


def rank_table(amount, slope):
    loads = [(1 << 20) // math.isqrt(rank ** slope) + 1 for rank in range(1, amount + 1)]
    width = 1 + sum(loads) // (1 << 30)
    return np.cumsum(np.array([max(1, weight // width) for weight in loads]))


def skewed_ids(rng, shape, count, lean):
    table = rank_table(count, lean)
    lot = jax.random.randint(jax.random.fold_in(rng, 1), shape, 0, int(table[count - 1]))
    rank = jnp.searchsorted(jnp.asarray(table, jnp.int32), lot, side="right")
    return jax.random.permutation(jax.random.fold_in(rng, 2), count)[rank].astype(jnp.int32)


def scatter_about(stream_key, shape, width, limit, cuts=(), held_as=jnp.bfloat16):
    array = width * jax.random.normal(stream_key, shape, jnp.float32)
    if cuts:
        array = array * block_levels(stream_key, shape, cuts, -0.22, 0.18)
    return jnp.clip(array, -limit, limit).astype(held_as)


def setup_inputs(seed: int = 0) -> dict:
    splits = jax.random.split(jax.random.key(seed), 15)
    flow_state = scatter_about(splits[0], (FLOWS, H), 1.0, 6.0, ((0, 32),))
    link_state = scatter_about(splits[1], (LINKS, H), 1.0, 6.0, ((0, 32),))
    incidence = scatter_about(splits[2], (LGROUPS, FGROUPS, TMAX, BS, BS), 0.05, 0.29882812, ((0, 4), (1, 8)))
    tile_flow = set_ends(jax.random.randint(splits[3], (LGROUPS, FGROUPS, TMAX), 0, FGB), jax.random.fold_in(splits[3], 1), 0, FGB - 1).astype(jnp.int32)
    tile_link = set_ends(skewed_ids(splits[4], (LGROUPS, FGROUPS, TMAX), LGB, 2), jax.random.fold_in(splits[4], 3), 0, LGB - 1).astype(jnp.int32)
    tile_live = draw_tile_live(jax.random.fold_in(splits[14], 71), 0)
    link_gain = jnp.clip(jnp.exp(jax.random.uniform(splits[6], (H,), jnp.float32, math.log(0.5), math.log(2.0))), 0.5, 2.0)
    link_agg_weight = scatter_about(splits[7], (H, H), H ** -0.5, 0.375)
    link_self_weight = scatter_about(splits[8], (H, H), H ** -0.5, 0.375)
    link_out_weight = scatter_about(splits[9], (H, H), H ** -0.5, 0.375)
    flow_gain = jnp.clip(jnp.exp(jax.random.uniform(splits[10], (H,), jnp.float32, math.log(0.5), math.log(2.0))), 0.5, 2.0)
    flow_agg_weight = scatter_about(splits[11], (H, H), H ** -0.5, 0.375)
    flow_self_weight = scatter_about(splits[12], (H, H), H ** -0.5, 0.375)
    flow_out_weight = scatter_about(splits[13], (H, H), H ** -0.5, 0.375)
    return dict(flow_state=flow_state, link_state=link_state, incidence=incidence, tile_flow=tile_flow, tile_link=tile_link, tile_live=tile_live, link_gain=link_gain, link_agg_weight=link_agg_weight, link_self_weight=link_self_weight, link_out_weight=link_out_weight, flow_gain=flow_gain, flow_agg_weight=flow_agg_weight, flow_self_weight=flow_self_weight, flow_out_weight=flow_out_weight)


def state_update(totals, state, gain, agg_weight, self_weight, out_weight):
    scale = lax.rsqrt(lax.optimization_barrier(jnp.mean(totals * totals, axis=-1, keepdims=True)) + 1e-05)
    normed = (totals * scale * gain).astype(jnp.bfloat16)
    before = jnp.dot(normed, agg_weight, preferred_element_type=jnp.float32) + jnp.dot(state, self_weight, preferred_element_type=jnp.float32)
    hidden = jax.nn.silu(before).astype(jnp.bfloat16)
    return (state.astype(jnp.float32) + jnp.dot(hidden, out_weight, preferred_element_type=jnp.float32)).astype(jnp.bfloat16)

def block_sums(coefs, pieces, targets, live_slots, block_count, to_links):
    if to_links:
        products = jnp.einsum('tij,tih->tjh', coefs.astype(jnp.float32), pieces.astype(jnp.float32))
    else:
        products = jnp.einsum('tij,tjh->tih', coefs.astype(jnp.float32), pieces.astype(jnp.float32))
    select = (targets[None, :] == jnp.arange(block_count, dtype=jnp.int32)[:, None]).astype(jnp.float32)
    select = select * live_slots.astype(jnp.float32)[None, :]
    return jnp.dot(select, products.reshape(products.shape[0], -1), precision=lax.Precision.HIGHEST)

def rounded(term):
    return lax.optimization_barrier(term.astype(jnp.bfloat16)).astype(jnp.float32)

def reference(flow_state, link_state, incidence, tile_flow, tile_link, tile_live, link_gain, link_agg_weight, link_self_weight, link_out_weight, flow_gain, flow_agg_weight, flow_self_weight, flow_out_weight):
    flow_groups = flow_state.reshape(FGROUPS, FGB, BS, H)

    def link_group_sum(link_index):

        def add_group(total, flow_index):
            pieces = jnp.take(flow_groups[flow_index], tile_flow[link_index, flow_index], axis=0)
            term = block_sums(incidence[link_index, flow_index], pieces, tile_link[link_index, flow_index], tile_live[link_index, flow_index], LGB, True)
            return (total + rounded(term), None)
        total, _ = lax.scan(add_group, jnp.zeros((LGB, BS * H), jnp.float32), jnp.arange(FGROUPS, dtype=jnp.int32))
        return total
    link_sum = lax.map(link_group_sum, jnp.arange(LGROUPS, dtype=jnp.int32)).reshape(LINKS, H)
    link_next = state_update(link_sum, link_state, link_gain, link_agg_weight, link_self_weight, link_out_weight)
    link_groups = link_next.reshape(LGROUPS, LGB, BS, H)

    def flow_group_sum(flow_index):

        def add_group(total, link_index):
            pieces = jnp.take(link_groups[link_index], tile_link[link_index, flow_index], axis=0)
            term = block_sums(incidence[link_index, flow_index], pieces, tile_flow[link_index, flow_index], tile_live[link_index, flow_index], FGB, False)
            return (total + rounded(term), None)
        total, _ = lax.scan(add_group, jnp.zeros((FGB, BS * H), jnp.float32), jnp.arange(LGROUPS, dtype=jnp.int32))
        return total
    flow_sum = lax.map(flow_group_sum, jnp.arange(FGROUPS, dtype=jnp.int32)).reshape(FLOWS, H)
    flow_next = state_update(flow_sum, flow_state, flow_gain, flow_agg_weight, flow_self_weight, flow_out_weight)
    return (link_next, flow_next)
```

```python
import functools

import jax
import jax.numpy as jnp
from jax import lax
from jax.experimental import pallas as pl
from jax.experimental.pallas import tpu as pltpu
from jax.sharding import PartitionSpec as P

H = 256
BS = 128
HALVES = 2
W = H // HALVES
MESH = pl.DeviceIdType.MESH


def sort_pairs(n):
    pairs = []
    p = 1
    while p < n:
        k = p
        while k >= 1:
            for j in range(k % p, n - k, 2 * k):
                for i in range(min(k, n - j - k)):
                    if (i + j) // (2 * p) == (i + j + k) // (2 * p):
                        pairs.append((i + j, i + j + k))
            k //= 2
        p *= 2
    return pairs


def order_slots(targets, sources, live, blocks, keys, ends):
    slots = targets.shape[2]
    held = []
    for s in range(slots):
        target = jnp.where(live[0, 0, s] == 1, targets[0, 0, s], blocks)
        held.append(target * 65536 + sources[0, 0, s] * 256 + s)
    for low, high in sort_pairs(slots):
        least, most = jnp.minimum(held[low], held[high]), jnp.maximum(held[low], held[high])
        held[low], held[high] = least, most
    keys[0] = jnp.int32(-1)
    for k in range(slots):
        keys[1 + k] = held[k]

    def count(b, carry):
        bound = (b + 1) * 65536
        below = jnp.int32(0)
        for k in range(slots):
            below = below + jnp.where(keys[1 + k] < bound, 1, 0)
        last = jnp.maximum(below - 1, 0)
        there = jnp.where(below > 0, jnp.where(lax.shift_right_logical(keys[1 + last], 16) == b, 1, 0), 0)
        ends[b] = last * 2 + there
        return carry

    lax.fori_loop(0, blocks, count, 0)


def segment_sums(slots, keys, ends, blocks, tile_of, source, sums, parts, half):
    unroll = 8 if slots % 8 == 0 else 1

    def steps(group, total):
        for inner in range(unroll):
            k = group * unroll + inner
            key = keys[1 + k]
            same = lax.shift_right_arithmetic(key, 16) == lax.shift_right_arithmetic(keys[k], 16)
            keep = jnp.where(same, 1.0, 0.0).astype(jnp.float32)
            piece = source[lax.shift_right_logical(key, 8) & 255]
            total = total * keep + jnp.dot(
                tile_of(k, key), piece, preferred_element_type=jnp.float32
            )
            sums[k] = total
        return total

    lax.fori_loop(0, slots // unroll, steps, jnp.zeros((BS, W), jnp.float32))

    def pick(b, carry):
        end = ends[b]
        there = jnp.where((end & 1) == 1, 1.0, 0.0).astype(jnp.float32)
        parts[half, b] = (sums[lax.shift_right_logical(end, 1)] * there).astype(jnp.bfloat16)
        return carry

    lax.fori_loop(0, blocks, pick, 0)


def updated(totals, state, own, gain, agg_weight, out_weight):
    square = sum(jnp.sum(t * t, axis=-1, keepdims=True) for t in totals)
    scale = lax.rsqrt(square * (1.0 / H) + 1e-05)
    before = own
    for half in range(HALVES):
        cut = slice(half * W, (half + 1) * W)
        normed = (totals[half] * scale * gain[:, cut]).astype(jnp.bfloat16)
        before = before + jnp.dot(normed, agg_weight[cut, :], preferred_element_type=jnp.float32)
    hidden = (before / (1.0 + jnp.exp(-before))).astype(jnp.bfloat16)
    return (
        state.astype(jnp.float32) + jnp.dot(hidden, out_weight[...], preferred_element_type=jnp.float32)
    ).astype(jnp.bfloat16)


def kernel(
    rows,
    cols,
    flow_state_hbm,
    link_state_hbm,
    coefs_hbm,
    link_agg_hbm,
    link_self_hbm,
    link_out_hbm,
    flow_agg_hbm,
    flow_self_hbm,
    flow_out_hbm,
    tile_flow,
    tile_link,
    tile_live,
    link_gain,
    flow_gain,
    link_next,
    flow_next,
    flow_state,
    link_state,
    coefs,
    link_agg,
    link_self,
    link_out,
    flow_agg,
    flow_self,
    flow_out,
    flows0,
    flows1,
    links0,
    links1,
    link_parts,
    link_in,
    flow_parts,
    flow_in,
    turned,
    sums,
    link_own,
    flow_own,
    link_keys,
    link_ends,
    flow_keys,
    flow_ends,
    send1,
    recv1,
    send2,
    recv2,
    send3,
    recv3,
    send4,
    recv4,
    own_sem,
    in_sem,
):
    flows, links = (flows0, flows1), (links0, links1)
    r, c = lax.axis_index("row"), lax.axis_index("col")
    slots = coefs.shape[2]
    fb, lb = flow_state.shape[0] // BS, link_state.shape[0] // BS
    flow_blocks, link_blocks = fb * rows, lb * cols

    def row_peer(t):
        return lax.rem(r + t, rows)

    def col_peer(t):
        return lax.rem(c + t, cols)

    def gather1(h, t):
        mine = flows[h].at[pl.ds(r * fb, fb)]
        return pltpu.make_async_remote_copy(
            src_ref=mine, dst_ref=mine, send_sem=send1.at[h, t], recv_sem=recv1.at[h, t],
            device_id=(row_peer(t), c), device_id_type=MESH,
        )

    def scatter2(h, t):
        peer = col_peer(t)
        return pltpu.make_async_remote_copy(
            src_ref=link_parts.at[h, pl.ds(peer * lb, lb)], dst_ref=link_in.at[h, t],
            send_sem=send2.at[h, t], recv_sem=recv2.at[h, t],
            device_id=(r, peer), device_id_type=MESH,
        )

    def gather3(h, t):
        mine = links[h].at[pl.ds(c * lb, lb)]
        return pltpu.make_async_remote_copy(
            src_ref=mine, dst_ref=mine, send_sem=send3.at[h, t], recv_sem=recv3.at[h, t],
            device_id=(r, col_peer(t)), device_id_type=MESH,
        )

    def scatter4(h, t):
        peer = row_peer(t)
        return pltpu.make_async_remote_copy(
            src_ref=flow_parts.at[h, pl.ds(peer * fb, fb)], dst_ref=flow_in.at[h, t],
            send_sem=send4.at[h, t], recv_sem=recv4.at[h, t],
            device_id=(peer, c), device_id_type=MESH,
        )

    row_steps, col_steps = range(1, rows), range(1, cols)
    barrier = pltpu.get_barrier_semaphore()
    for t in row_steps:
        pl.semaphore_signal(barrier, inc=1, device_id=(row_peer(t), c), device_id_type=MESH)
    for t in col_steps:
        pl.semaphore_signal(barrier, inc=1, device_id=(r, col_peer(t)), device_id_type=MESH)
    own_in = [
        pltpu.make_async_copy(
            flow_state_hbm.at[pl.ds(b * BS, BS), pl.ds(h * W, W)], flows[h].at[r * fb + b], own_sem.at[h, b]
        )
        for h in range(HALVES)
        for b in range(fb)
    ]
    pairs = (
        (coefs_hbm, coefs),
        (link_state_hbm, link_state),
        (link_self_hbm, link_self),
        (flow_state_hbm, flow_state),
        (flow_self_hbm, flow_self),
        (link_agg_hbm, link_agg),
        (link_out_hbm, link_out),
        (flow_agg_hbm, flow_agg),
        (flow_out_hbm, flow_out),
    )
    operands_in = [pltpu.make_async_copy(a, b, in_sem.at[n]) for n, (a, b) in enumerate(pairs)]
    for copy in own_in + operands_in:
        copy.start()
    for copy in own_in:
        copy.wait()
    pl.semaphore_wait(barrier, rows + cols - 2)

    for h in range(HALVES):
        for t in row_steps:
            gather1(h, t).start()

    order_slots(tile_link, tile_flow, tile_live, link_blocks, link_keys, link_ends)
    order_slots(tile_flow, tile_link, tile_live, flow_blocks, flow_keys, flow_ends)

    for copy in operands_in:
        copy.wait()

    def turn(k, carry):
        turned[k] = coefs[0, 0, link_keys[1 + k] & 255].T
        return carry

    lax.fori_loop(0, slots, turn, 0)
    link_own[...] = jnp.dot(link_state[...], link_self[...], preferred_element_type=jnp.float32)
    flow_own[...] = jnp.dot(flow_state[...], flow_self[...], preferred_element_type=jnp.float32)

    for h in range(HALVES):
        for t in row_steps:
            gather1(h, t).wait_recv()
        segment_sums(
            slots, link_keys, link_ends, link_blocks, lambda k, key: turned[k], flows[h], sums, link_parts, h
        )
        for t in col_steps:
            scatter2(h, t).start()

    totals = []
    for h in range(HALVES):
        total = link_parts[h, pl.ds(c * lb, lb)].astype(jnp.float32)
        for t in col_steps:
            scatter2(h, t).wait_recv()
            total = total + link_in[h, t].astype(jnp.float32)
        totals.append(total.reshape(lb * BS, W))
    fresh = updated(totals, link_state[...], link_own[...], link_gain, link_agg, link_out)
    for h in range(HALVES):
        for b in range(lb):
            links[h][c * lb + b] = fresh[b * BS : (b + 1) * BS, h * W : (h + 1) * W]
        for t in col_steps:
            gather3(h, t).start()
    link_next[...] = fresh

    for h in range(HALVES):
        for t in col_steps:
            gather3(h, t).wait_recv()
        segment_sums(
            slots, flow_keys, flow_ends, flow_blocks, lambda k, key: coefs[0, 0, key & 255], links[h], sums, flow_parts, h
        )
        for t in row_steps:
            scatter4(h, t).start()

    totals = []
    for h in range(HALVES):
        total = flow_parts[h, pl.ds(r * fb, fb)].astype(jnp.float32)
        for t in row_steps:
            scatter4(h, t).wait_recv()
            total = total + flow_in[h, t].astype(jnp.float32)
        totals.append(total.reshape(fb * BS, W))
    flow_next[...] = updated(totals, flow_state[...], flow_own[...], flow_gain, flow_agg, flow_out)

    for h in range(HALVES):
        for t in row_steps:
            gather1(h, t).wait_send()
            scatter4(h, t).wait_send()
        for t in col_steps:
            scatter2(h, t).wait_send()
            gather3(h, t).wait_send()


def on_device(
    rows,
    cols,
    flow_state,
    link_state,
    incidence,
    tile_flow,
    tile_link,
    tile_live,
    link_gain,
    link_agg_weight,
    link_self_weight,
    link_out_weight,
    flow_gain,
    flow_agg_weight,
    flow_self_weight,
    flow_out_weight,
):
    slots = incidence.shape[2]
    fb, lb = flow_state.shape[0] // BS, link_state.shape[0] // BS
    flow_blocks, link_blocks = fb * rows, lb * cols
    vmem = pl.BlockSpec(memory_space=pltpu.VMEM)
    hbm = pl.BlockSpec(memory_space=pl.ANY)
    smem = pl.BlockSpec(memory_space=pltpu.SMEM)
    bf16, f32, i32 = jnp.bfloat16, jnp.float32, jnp.int32
    dma = pltpu.SemaphoreType.DMA
    return pl.pallas_call(
        functools.partial(kernel, rows, cols),
        out_shape=(
            jax.ShapeDtypeStruct(link_state.shape, bf16),
            jax.ShapeDtypeStruct(flow_state.shape, bf16),
        ),
        in_specs=[hbm] * 9 + [smem] * 3 + [vmem] * 2,
        out_specs=(vmem, vmem),
        scratch_shapes=[
            pltpu.VMEM(flow_state.shape, bf16),
            pltpu.VMEM(link_state.shape, bf16),
            pltpu.VMEM(incidence.shape, bf16),
            *[pltpu.VMEM((H, H), bf16) for _ in range(6)],
            *[pltpu.VMEM((flow_blocks, BS, W), bf16) for _ in range(HALVES)],
            *[pltpu.VMEM((link_blocks, BS, W), bf16) for _ in range(HALVES)],
            pltpu.VMEM((HALVES, link_blocks, BS, W), bf16),
            pltpu.VMEM((HALVES, cols, lb, BS, W), bf16),
            pltpu.VMEM((HALVES, flow_blocks, BS, W), bf16),
            pltpu.VMEM((HALVES, rows, fb, BS, W), bf16),
            pltpu.VMEM((slots, BS, BS), bf16),
            pltpu.VMEM((slots, BS, W), f32),
            pltpu.VMEM((lb * BS, H), f32),
            pltpu.VMEM((fb * BS, H), f32),
            pltpu.SMEM((slots + 1,), i32),
            pltpu.SMEM((link_blocks,), i32),
            pltpu.SMEM((slots + 1,), i32),
            pltpu.SMEM((flow_blocks,), i32),
            dma((HALVES, rows)),
            dma((HALVES, rows)),
            dma((HALVES, cols)),
            dma((HALVES, cols)),
            dma((HALVES, cols)),
            dma((HALVES, cols)),
            dma((HALVES, rows)),
            dma((HALVES, rows)),
            dma((HALVES, fb)),
            dma((9,)),
        ],
        compiler_params=pltpu.CompilerParams(
            collective_id=0, has_side_effects=True, vmem_limit_bytes=40 * 1024 * 1024
        ),
        name="message_round",
    )(
        flow_state,
        link_state,
        incidence,
        link_agg_weight,
        link_self_weight,
        link_out_weight,
        flow_agg_weight,
        flow_self_weight,
        flow_out_weight,
        tile_flow,
        tile_link,
        tile_live,
        link_gain.reshape(1, H),
        flow_gain.reshape(1, H),
    )


def solution(mesh):
    return jax.shard_map(
        functools.partial(on_device, mesh.shape["row"], mesh.shape["col"]),
        mesh=mesh,
        in_specs=(
            P(("col", "row"), None),
            P(("row", "col"), None),
            P("row", "col", None, None, None),
            P("row", "col", None),
            P("row", "col", None),
            P("row", "col", None),
            P(),
            P(),
            P(),
            P(),
            P(),
            P(),
            P(),
            P(),
        ),
        out_specs=(P(("row", "col"), None), P(("col", "row"), None)),
        check_vma=False,
    )
```

```python
import functools

import jax
import jax.numpy as jnp
from jax import lax
from jax.experimental import pallas as pl
from jax.experimental.pallas import tpu as pltpu
from jax.sharding import PartitionSpec as P

H = 256
BS = 128
HALVES = 2
W = H // HALVES
MESH = pl.DeviceIdType.MESH


def sort_pairs(n):
    pairs = []
    p = 1
    while p < n:
        k = p
        while k >= 1:
            for j in range(k % p, n - k, 2 * k):
                for i in range(min(k, n - j - k)):
                    if (i + j) // (2 * p) == (i + j + k) // (2 * p):
                        pairs.append((i + j, i + j + k))
            k //= 2
        p *= 2
    return pairs


def order_slots(targets, sources, live, blocks, keys, ends):
    slots = targets.shape[2]
    held = []
    for s in range(slots):
        target = jnp.where(live[0, 0, s] == 1, targets[0, 0, s], blocks)
        held.append(target * 65536 + sources[0, 0, s] * 256 + s)
    for low, high in sort_pairs(slots):
        least, most = jnp.minimum(held[low], held[high]), jnp.maximum(held[low], held[high])
        held[low], held[high] = least, most
    keys[0] = jnp.int32(-1)
    for k in range(slots):
        keys[1 + k] = held[k]

    def count(b, carry):
        bound = (b + 1) * 65536
        below = jnp.int32(0)
        for k in range(slots):
            below = below + jnp.where(keys[1 + k] < bound, 1, 0)
        last = jnp.maximum(below - 1, 0)
        there = jnp.where(below > 0, jnp.where(lax.shift_right_logical(keys[1 + last], 16) == b, 1, 0), 0)
        ends[b] = last * 2 + there
        return carry

    lax.fori_loop(0, blocks, count, 0)


def segment_sums(slots, keys, ends, blocks, tile_of, source, sums, parts, half):
    unroll = 8 if slots % 8 == 0 else 1

    def steps(group, total):
        for inner in range(unroll):
            k = group * unroll + inner
            key = keys[1 + k]
            same = lax.shift_right_arithmetic(key, 16) == lax.shift_right_arithmetic(keys[k], 16)
            keep = jnp.where(same, 1.0, 0.0).astype(jnp.float32)
            piece = source[lax.shift_right_logical(key, 8) & 255]
            total = total * keep + jnp.dot(
                tile_of(k, key), piece, preferred_element_type=jnp.float32
            )
            sums[k] = total
        return total

    lax.fori_loop(0, slots // unroll, steps, jnp.zeros((BS, W), jnp.float32))

    def pick(b, carry):
        end = ends[b]
        there = jnp.where((end & 1) == 1, 1.0, 0.0).astype(jnp.float32)
        parts[half, b] = (sums[lax.shift_right_logical(end, 1)] * there).astype(jnp.bfloat16)
        return carry

    lax.fori_loop(0, blocks, pick, 0)


def updated(totals, state, own, gain, agg_weight, out_weight):
    square = sum(jnp.sum(t * t, axis=-1, keepdims=True) for t in totals)
    scale = lax.rsqrt(square * (1.0 / H) + 1e-05)
    before = own
    for half in range(HALVES):
        cut = slice(half * W, (half + 1) * W)
        normed = (totals[half] * scale * gain[:, cut]).astype(jnp.bfloat16)
        before = before + jnp.dot(normed, agg_weight[cut, :], preferred_element_type=jnp.float32)
    hidden = (before / (1.0 + jnp.exp(-before))).astype(jnp.bfloat16)
    return (
        state.astype(jnp.float32) + jnp.dot(hidden, out_weight[...], preferred_element_type=jnp.float32)
    ).astype(jnp.bfloat16)


def kernel(
    rows,
    cols,
    flow_state_hbm,
    link_state_hbm,
    coefs_hbm,
    link_agg_hbm,
    link_self_hbm,
    link_out_hbm,
    flow_agg_hbm,
    flow_self_hbm,
    flow_out_hbm,
    tile_flow_hbm,
    tile_link_hbm,
    tile_live_hbm,
    link_gain_hbm,
    flow_gain_hbm,
    link_next,
    flow_next,
    flow_state,
    link_state,
    coefs,
    link_agg,
    link_self,
    link_out,
    flow_agg,
    flow_self,
    flow_out,
    link_gain,
    flow_gain,
    tile_flow,
    tile_link,
    tile_live,
    flows0,
    flows1,
    links0,
    links1,
    link_parts,
    link_in,
    flow_parts,
    flow_in,
    turned,
    sums,
    link_own,
    flow_own,
    link_keys,
    link_ends,
    flow_keys,
    flow_ends,
    send1,
    recv1,
    send2,
    recv2,
    send3,
    recv3,
    send4,
    recv4,
    own_sem,
    in_sem,
    relay_in,
    relay_send1,
    relay_send4,
    relay_recv4,
):
    flows, links = (flows0, flows1), (links0, links1)
    r, c = lax.axis_index("row"), lax.axis_index("col")
    slots = coefs.shape[2]
    fb, lb = flow_state.shape[0] // BS, link_state.shape[0] // BS
    flow_blocks, link_blocks = fb * rows, lb * cols

    def row_peer(t):
        return lax.rem(r + t, rows)

    def col_peer(t):
        return lax.rem(c + t, cols)

    def gather1(h, t):
        mine = flows[h].at[pl.ds(r * fb, fb)]
        return pltpu.make_async_remote_copy(
            src_ref=mine, dst_ref=mine, send_sem=send1.at[h, t], recv_sem=recv1.at[h, t],
            device_id=(row_peer(t), c), device_id_type=MESH,
        )

    def scatter2(h, t):
        peer = col_peer(t)
        return pltpu.make_async_remote_copy(
            src_ref=link_parts.at[h, pl.ds(peer * lb, lb)], dst_ref=link_in.at[h, t],
            send_sem=send2.at[h, t], recv_sem=recv2.at[h, t],
            device_id=(r, peer), device_id_type=MESH,
        )

    def gather3(h, t):
        mine = links[h].at[pl.ds(c * lb, lb)]
        return pltpu.make_async_remote_copy(
            src_ref=mine, dst_ref=mine, send_sem=send3.at[h, t], recv_sem=recv3.at[h, t],
            device_id=(r, col_peer(t)), device_id_type=MESH,
        )

    def scatter4(h, t):
        peer = row_peer(t)
        return pltpu.make_async_remote_copy(
            src_ref=flow_parts.at[h, pl.ds(peer * fb, fb)], dst_ref=flow_in.at[h, t],
            send_sem=send4.at[h, t], recv_sem=recv4.at[h, t],
            device_id=(peer, c), device_id_type=MESH,
        )

    last = rows - 1
    ways = ((0, 1, rows - 2, last), (last, last - 1, 1, 0)) if rows > 2 else ()

    def relay1(h, way):
        begin, _, near, end = ways[way]
        shard = flows[h].at[pl.ds(begin * fb, fb)]
        return pltpu.make_async_remote_copy(
            src_ref=shard, dst_ref=shard, send_sem=relay_send1.at[h, way],
            recv_sem=recv1.at[h, (end - begin) % rows],
            device_id=(end, c), device_id_type=MESH,
        )

    def relay4(h, way):
        begin, near, _, end = ways[way]
        return pltpu.make_async_remote_copy(
            src_ref=flow_parts.at[h, pl.ds(end * fb, fb)], dst_ref=relay_in.at[h, way],
            send_sem=relay_send4.at[h, way], recv_sem=relay_recv4.at[h, way],
            device_id=(near, c), device_id_type=MESH,
        )

    def unless(places, act):
        if not places:
            act()
            return
        free = r != places[0]
        for place in places[1:]:
            free = jnp.logical_and(free, r != place)
        pl.when(free)(act)

    def ends_of(t):
        return [begin for begin, _, _, end in ways if (end - begin) % rows == t]

    def met(t):
        return [end for begin, _, _, end in ways if (end - begin) % rows == t]

    def passed1(t):
        return [near for begin, _, near, _ in ways if (near - begin) % rows == t]

    def joined4(t):
        return [near for _, near, _, end in ways if (end - near) % rows == t]

    row_steps = sorted(range(1, rows), key=lambda t: (-min(t, rows - t), t))
    col_steps = range(1, cols)
    barrier = pltpu.get_barrier_semaphore()
    for t in row_steps:
        pl.semaphore_signal(barrier, inc=1, device_id=(row_peer(t), c), device_id_type=MESH)
    for t in col_steps:
        pl.semaphore_signal(barrier, inc=1, device_id=(r, col_peer(t)), device_id_type=MESH)
    own_in = [
        pltpu.make_async_copy(
            flow_state_hbm.at[pl.ds(b * BS, BS), pl.ds(h * W, W)], flows[h].at[r * fb + b], own_sem.at[h, b]
        )
        for h in range(HALVES)
        for b in range(fb)
    ]
    pairs = (
        (coefs_hbm, coefs),
        (link_state_hbm, link_state),
        (link_self_hbm, link_self),
        (flow_state_hbm, flow_state),
        (flow_self_hbm, flow_self),
        (link_agg_hbm, link_agg),
        (link_out_hbm, link_out),
        (flow_agg_hbm, flow_agg),
        (flow_out_hbm, flow_out),
        (link_gain_hbm, link_gain),
        (flow_gain_hbm, flow_gain),
    )
    tables = (
        (tile_flow_hbm, tile_flow),
        (tile_link_hbm, tile_link),
        (tile_live_hbm, tile_live),
    )
    tables_in = [pltpu.make_async_copy(a, b, in_sem.at[len(pairs) + n]) for n, (a, b) in enumerate(tables)]
    operands_in = [pltpu.make_async_copy(a, b, in_sem.at[n]) for n, (a, b) in enumerate(pairs)]
    for copy in own_in + tables_in + operands_in:
        copy.start()
    for copy in own_in:
        copy.wait()
    pl.semaphore_wait(barrier, rows + cols - 2)

    for h in range(HALVES):
        for t in row_steps:
            unless(ends_of(t), lambda: gather1(h, t).start())
    for h in range(HALVES):
        for way, (begin, _, _, end) in enumerate(ways):

            @pl.when(r == end)
            def _():
                flow_in[h, (end - begin) % rows] = jnp.zeros((fb, BS, W), jnp.bfloat16)

    for copy in tables_in:
        copy.wait()
    order_slots(tile_link, tile_flow, tile_live, link_blocks, link_keys, link_ends)
    order_slots(tile_flow, tile_link, tile_live, flow_blocks, flow_keys, flow_ends)

    for copy in operands_in:
        copy.wait()

    def turn(k, carry):
        turned[k] = coefs[0, 0, link_keys[1 + k] & 255].T
        return carry

    lax.fori_loop(0, slots, turn, 0)
    link_own[...] = jnp.dot(link_state[...], link_self[...], preferred_element_type=jnp.float32)
    flow_own[...] = jnp.dot(flow_state[...], flow_self[...], preferred_element_type=jnp.float32)

    for h in range(HALVES):
        for way, (begin, _, near, _) in enumerate(ways):

            @pl.when(r == near)
            def _():
                gather1(h, (near - begin) % rows).wait_recv()
                relay1(h, way).start()

    for h in range(HALVES):
        for t in row_steps:
            unless(passed1(t), lambda: gather1(h, t).wait_recv())
        segment_sums(
            slots, link_keys, link_ends, link_blocks, lambda k, key: turned[k], flows[h], sums, link_parts, h
        )
        for t in col_steps:
            scatter2(h, t).start()

    totals = []
    for h in range(HALVES):
        total = link_parts[h, pl.ds(c * lb, lb)].astype(jnp.float32)
        for t in col_steps:
            scatter2(h, t).wait_recv()
            total = total + link_in[h, t].astype(jnp.float32)
        totals.append(total.reshape(lb * BS, W))
    fresh = updated(totals, link_state[...], link_own[...], link_gain, link_agg, link_out)
    for h in range(HALVES):
        for b in range(lb):
            links[h][c * lb + b] = fresh[b * BS : (b + 1) * BS, h * W : (h + 1) * W]
        for t in col_steps:
            gather3(h, t).start()
    link_next[...] = fresh

    for h in range(HALVES):
        for t in col_steps:
            gather3(h, t).wait_recv()
        segment_sums(
            slots, flow_keys, flow_ends, flow_blocks, lambda k, key: coefs[0, 0, key & 255], links[h], sums, flow_parts, h
        )
        for way, (begin, _, _, _) in enumerate(ways):
            pl.when(r == begin)(lambda: relay4(h, way).start())
        for t in row_steps:
            unless(ends_of(t) + joined4(t), lambda: scatter4(h, t).start())
    for h in range(HALVES):
        for way, (_, near, _, end) in enumerate(ways):

            @pl.when(r == near)
            def _():
                relay4(h, way).wait_recv()
                part = flow_parts[h, pl.ds(end * fb, fb)].astype(jnp.float32)
                part = part + relay_in[h, way].astype(jnp.float32)
                flow_parts[h, pl.ds(end * fb, fb)] = part.astype(jnp.bfloat16)
                scatter4(h, (end - near) % rows).start()

    totals = []
    for h in range(HALVES):
        total = flow_parts[h, pl.ds(r * fb, fb)].astype(jnp.float32)
        for t in row_steps:
            unless(met(t), lambda: scatter4(h, t).wait_recv())
            total = total + flow_in[h, t].astype(jnp.float32)
        totals.append(total.reshape(fb * BS, W))
    flow_next[...] = updated(totals, flow_state[...], flow_own[...], flow_gain, flow_agg, flow_out)

    for h in range(HALVES):
        for t in row_steps:
            unless(ends_of(t), lambda: gather1(h, t).wait_send())
            unless(ends_of(t), lambda: scatter4(h, t).wait_send())
        for way, (begin, _, near, _) in enumerate(ways):
            pl.when(r == near)(lambda: relay1(h, way).wait_send())
            pl.when(r == begin)(lambda: relay4(h, way).wait_send())
        for t in col_steps:
            scatter2(h, t).wait_send()
            gather3(h, t).wait_send()


def on_device(
    rows,
    cols,
    flow_state,
    link_state,
    incidence,
    tile_flow,
    tile_link,
    tile_live,
    link_gain,
    link_agg_weight,
    link_self_weight,
    link_out_weight,
    flow_gain,
    flow_agg_weight,
    flow_self_weight,
    flow_out_weight,
):
    slots = incidence.shape[2]
    fb, lb = flow_state.shape[0] // BS, link_state.shape[0] // BS
    flow_blocks, link_blocks = fb * rows, lb * cols
    vmem = pl.BlockSpec(memory_space=pltpu.VMEM)
    hbm = pl.BlockSpec(memory_space=pltpu.HBM)
    bf16, f32, i32 = jnp.bfloat16, jnp.float32, jnp.int32
    dma = pltpu.SemaphoreType.DMA
    return pl.pallas_call(
        functools.partial(kernel, rows, cols),
        out_shape=(
            jax.ShapeDtypeStruct(link_state.shape, bf16),
            jax.ShapeDtypeStruct(flow_state.shape, bf16),
        ),
        in_specs=[hbm] * 14,
        out_specs=(vmem, vmem),
        scratch_shapes=[
            pltpu.VMEM(flow_state.shape, bf16),
            pltpu.VMEM(link_state.shape, bf16),
            pltpu.VMEM(incidence.shape, bf16),
            *[pltpu.VMEM((H, H), bf16) for _ in range(6)],
            *[pltpu.VMEM((1, H), f32) for _ in range(2)],
            *[pltpu.SMEM((1, 1, slots), i32) for _ in range(3)],
            *[pltpu.VMEM((flow_blocks, BS, W), bf16) for _ in range(HALVES)],
            *[pltpu.VMEM((link_blocks, BS, W), bf16) for _ in range(HALVES)],
            pltpu.VMEM((HALVES, link_blocks, BS, W), bf16),
            pltpu.VMEM((HALVES, cols, lb, BS, W), bf16),
            pltpu.VMEM((HALVES, flow_blocks, BS, W), bf16),
            pltpu.VMEM((HALVES, rows, fb, BS, W), bf16),
            pltpu.VMEM((slots, BS, BS), bf16),
            pltpu.VMEM((slots, BS, W), f32),
            pltpu.VMEM((lb * BS, H), f32),
            pltpu.VMEM((fb * BS, H), f32),
            pltpu.SMEM((slots + 1,), i32),
            pltpu.SMEM((link_blocks,), i32),
            pltpu.SMEM((slots + 1,), i32),
            pltpu.SMEM((flow_blocks,), i32),
            dma((HALVES, rows)),
            dma((HALVES, rows)),
            dma((HALVES, cols)),
            dma((HALVES, cols)),
            dma((HALVES, cols)),
            dma((HALVES, cols)),
            dma((HALVES, rows)),
            dma((HALVES, rows)),
            dma((HALVES, fb)),
            dma((14,)),
            pltpu.VMEM((HALVES, 2, fb, BS, W), bf16),
            dma((HALVES, 2)),
            dma((HALVES, 2)),
            dma((HALVES, 2)),
        ],
        compiler_params=pltpu.CompilerParams(
            collective_id=0, has_side_effects=True, vmem_limit_bytes=60 * 1024 * 1024
        ),
        name="message_round",
    )(
        flow_state,
        link_state,
        incidence,
        link_agg_weight,
        link_self_weight,
        link_out_weight,
        flow_agg_weight,
        flow_self_weight,
        flow_out_weight,
        tile_flow,
        tile_link,
        tile_live,
        link_gain.reshape(1, H),
        flow_gain.reshape(1, H),
    )


def solution(mesh):
    return jax.shard_map(
        functools.partial(on_device, mesh.shape["row"], mesh.shape["col"]),
        mesh=mesh,
        in_specs=(
            P(("col", "row"), None),
            P(("row", "col"), None),
            P("row", "col", None, None, None),
            P("row", "col", None),
            P("row", "col", None),
            P("row", "col", None),
            P(),
            P(),
            P(),
            P(),
            P(),
            P(),
            P(),
            P(),
        ),
        out_specs=(P(("row", "col"), None), P(("col", "row"), None)),
        check_vma=False,
    )
```

```python
import functools

import jax
import jax.numpy as jnp
from jax import lax
from jax.experimental import pallas as pl
from jax.experimental.pallas import tpu as pltpu
from jax.sharding import PartitionSpec as P

H = 256
BS = 128
HALVES = 2
W = H // HALVES
MESH = pl.DeviceIdType.MESH


def sort_pairs(n):
    pairs = []
    p = 1
    while p < n:
        k = p
        while k >= 1:
            for j in range(k % p, n - k, 2 * k):
                for i in range(min(k, n - j - k)):
                    if (i + j) // (2 * p) == (i + j + k) // (2 * p):
                        pairs.append((i + j, i + j + k))
            k //= 2
        p *= 2
    return pairs


def order_slots(targets, sources, live, blocks, keys, ends):
    slots = targets.shape[2]
    held = []
    for s in range(slots):
        target = jnp.where(live[0, 0, s] == 1, targets[0, 0, s], blocks)
        held.append(target * 65536 + sources[0, 0, s] * 256 + s)
    for low, high in sort_pairs(slots):
        least, most = jnp.minimum(held[low], held[high]), jnp.maximum(held[low], held[high])
        held[low], held[high] = least, most
    keys[0] = jnp.int32(-1)
    for k in range(slots):
        keys[1 + k] = held[k]

    def count(b, carry):
        bound = (b + 1) * 65536
        below = jnp.int32(0)
        for k in range(slots):
            below = below + jnp.where(keys[1 + k] < bound, 1, 0)
        last = jnp.maximum(below - 1, 0)
        there = jnp.where(below > 0, jnp.where(lax.shift_right_logical(keys[1 + last], 16) == b, 1, 0), 0)
        ends[b] = last * 2 + there
        return carry

    lax.fori_loop(0, blocks, count, 0)


def segment_sums(slots, keys, ends, blocks, tile_of, source, sums, parts, half):
    unroll = 8 if slots % 8 == 0 else 1

    def steps(group, total):
        for inner in range(unroll):
            k = group * unroll + inner
            key = keys[1 + k]
            same = lax.shift_right_arithmetic(key, 16) == lax.shift_right_arithmetic(keys[k], 16)
            keep = jnp.where(same, 1.0, 0.0).astype(jnp.float32)
            piece = source[lax.shift_right_logical(key, 8) & 255]
            total = total * keep + jnp.dot(
                tile_of(k, key), piece, preferred_element_type=jnp.float32
            )
            sums[k] = total
        return total

    lax.fori_loop(0, slots // unroll, steps, jnp.zeros((BS, W), jnp.float32))

    def pick(b, carry):
        end = ends[b]
        there = jnp.where((end & 1) == 1, 1.0, 0.0).astype(jnp.float32)
        parts[half, b] = (sums[lax.shift_right_logical(end, 1)] * there).astype(jnp.bfloat16)
        return carry

    lax.fori_loop(0, blocks, pick, 0)


def updated(totals, state, own, gain, agg_weight, out_weight):
    square = sum(jnp.sum(t * t, axis=-1, keepdims=True) for t in totals)
    scale = lax.rsqrt(square * (1.0 / H) + 1e-05)
    before = own
    for half in range(HALVES):
        cut = slice(half * W, (half + 1) * W)
        normed = (totals[half] * scale * gain[:, cut]).astype(jnp.bfloat16)
        before = before + jnp.dot(normed, agg_weight[cut, :], preferred_element_type=jnp.float32)
    hidden = (before / (1.0 + jnp.exp(-before))).astype(jnp.bfloat16)
    return (
        state.astype(jnp.float32) + jnp.dot(hidden, out_weight[...], preferred_element_type=jnp.float32)
    ).astype(jnp.bfloat16)


def kernel(
    rows,
    cols,
    flow_state_hbm,
    link_state_hbm,
    coefs_hbm,
    link_agg_hbm,
    link_self_hbm,
    link_out_hbm,
    flow_agg_hbm,
    flow_self_hbm,
    flow_out_hbm,
    tile_flow_hbm,
    tile_link_hbm,
    tile_live_hbm,
    link_gain_hbm,
    flow_gain_hbm,
    link_next,
    flow_next,
    flow_state,
    link_state,
    coefs,
    link_agg,
    link_self,
    link_out,
    flow_agg,
    flow_self,
    flow_out,
    link_gain,
    flow_gain,
    tile_flow,
    tile_link,
    tile_live,
    flows0,
    flows1,
    links0,
    links1,
    link_parts,
    link_in,
    flow_parts,
    flow_in,
    turned,
    sums,
    link_own,
    flow_own,
    link_keys,
    link_ends,
    flow_keys,
    flow_ends,
    send1,
    recv1,
    send2,
    recv2,
    send3,
    recv3,
    send4,
    recv4,
    own_sem,
    in_sem,
    relay_in,
    relay_send1,
    relay_send4,
    relay_recv4,
):
    flows, links = (flows0, flows1), (links0, links1)
    r, c = lax.axis_index("row"), lax.axis_index("col")
    slots = coefs.shape[2]
    fb, lb = flow_state.shape[0] // BS, link_state.shape[0] // BS
    flow_blocks, link_blocks = fb * rows, lb * cols

    def row_peer(t):
        return lax.rem(r + t, rows)

    def col_peer(t):
        return lax.rem(c + t, cols)

    def gather1(h, t):
        mine = flows[h].at[pl.ds(r * fb, fb)]
        return pltpu.make_async_remote_copy(
            src_ref=mine, dst_ref=mine, send_sem=send1.at[h, t], recv_sem=recv1.at[h, t],
            device_id=(row_peer(t), c), device_id_type=MESH,
        )

    def scatter2(h, t):
        peer = col_peer(t)
        return pltpu.make_async_remote_copy(
            src_ref=link_parts.at[h, pl.ds(peer * lb, lb)], dst_ref=link_in.at[h, t],
            send_sem=send2.at[h, t], recv_sem=recv2.at[h, t],
            device_id=(r, peer), device_id_type=MESH,
        )

    def gather3(h, t):
        mine = links[h].at[pl.ds(c * lb, lb)]
        return pltpu.make_async_remote_copy(
            src_ref=mine, dst_ref=mine, send_sem=send3.at[h, t], recv_sem=recv3.at[h, t],
            device_id=(r, col_peer(t)), device_id_type=MESH,
        )

    def scatter4(h, t):
        peer = row_peer(t)
        return pltpu.make_async_remote_copy(
            src_ref=flow_parts.at[h, pl.ds(peer * fb, fb)], dst_ref=flow_in.at[h, t],
            send_sem=send4.at[h, t], recv_sem=recv4.at[h, t],
            device_id=(peer, c), device_id_type=MESH,
        )

    last = rows - 1
    ways = ((0, 1, rows - 2, last), (last, last - 1, 1, 0)) if rows > 2 else ()

    def relay1(h, way):
        begin, _, near, end = ways[way]
        shard = flows[h].at[pl.ds(begin * fb, fb)]
        return pltpu.make_async_remote_copy(
            src_ref=shard, dst_ref=shard, send_sem=relay_send1.at[h, way],
            recv_sem=recv1.at[h, (end - begin) % rows],
            device_id=(end, c), device_id_type=MESH,
        )

    def relay4(h, way):
        begin, near, _, end = ways[way]
        return pltpu.make_async_remote_copy(
            src_ref=flow_parts.at[h, pl.ds(end * fb, fb)], dst_ref=relay_in.at[h, way],
            send_sem=relay_send4.at[h, way], recv_sem=relay_recv4.at[h, way],
            device_id=(near, c), device_id_type=MESH,
        )

    def unless(places, act):
        if not places:
            act()
            return
        free = r != places[0]
        for place in places[1:]:
            free = jnp.logical_and(free, r != place)
        pl.when(free)(act)

    def ends_of(t):
        return [begin for begin, _, _, end in ways if (end - begin) % rows == t]

    def met(t):
        return [end for begin, _, _, end in ways if (end - begin) % rows == t]

    def passed1(t):
        return [near for begin, _, near, _ in ways if (near - begin) % rows == t]

    def joined4(t):
        return [near for _, near, _, end in ways if (end - near) % rows == t]

    row_steps = sorted(range(1, rows), key=lambda t: (-min(t, rows - t), t))
    col_steps = range(1, cols)
    barrier = pltpu.get_barrier_semaphore()
    for t in row_steps:
        pl.semaphore_signal(barrier, inc=1, device_id=(row_peer(t), c), device_id_type=MESH)
    for t in col_steps:
        pl.semaphore_signal(barrier, inc=1, device_id=(r, col_peer(t)), device_id_type=MESH)
    own_in = [
        pltpu.make_async_copy(
            flow_state_hbm.at[pl.ds(b * BS, BS), pl.ds(h * W, W)], flows[h].at[r * fb + b], own_sem.at[h, b]
        )
        for h in range(HALVES)
        for b in range(fb)
    ]
    pairs = (
        (coefs_hbm, coefs),
        (link_state_hbm, link_state),
        (link_self_hbm, link_self),
        (flow_state_hbm, flow_state),
        (flow_self_hbm, flow_self),
        (link_agg_hbm, link_agg),
        (link_out_hbm, link_out),
        (flow_agg_hbm, flow_agg),
        (flow_out_hbm, flow_out),
        (link_gain_hbm, link_gain),
        (flow_gain_hbm, flow_gain),
    )
    tables = (
        (tile_flow_hbm, tile_flow),
        (tile_link_hbm, tile_link),
        (tile_live_hbm, tile_live),
    )
    tables_in = [pltpu.make_async_copy(a, b, in_sem.at[len(pairs) + n]) for n, (a, b) in enumerate(tables)]
    operands_in = [pltpu.make_async_copy(a, b, in_sem.at[n]) for n, (a, b) in enumerate(pairs)]
    for copy in own_in + tables_in + operands_in:
        copy.start()
    for copy in own_in:
        copy.wait()
    pl.semaphore_wait(barrier, rows + cols - 2)

    for t in row_steps:
        unless(ends_of(t), lambda: gather1(0, t).start())
    for h in range(HALVES):
        for way, (begin, _, _, end) in enumerate(ways):

            @pl.when(r == end)
            def _():
                flow_in[h, (end - begin) % rows] = jnp.zeros((fb, BS, W), jnp.bfloat16)

    for copy in tables_in:
        copy.wait()
    order_slots(tile_link, tile_flow, tile_live, link_blocks, link_keys, link_ends)
    order_slots(tile_flow, tile_link, tile_live, flow_blocks, flow_keys, flow_ends)

    for h in range(1, HALVES):
        for t in row_steps:
            unless(ends_of(t), lambda: gather1(h - 1, t).wait_send())
        for t in row_steps:
            unless(ends_of(t), lambda: gather1(h, t).start())
    for copy in operands_in:
        copy.wait()

    def turn(k, carry):
        turned[k] = coefs[0, 0, link_keys[1 + k] & 255].T
        return carry

    lax.fori_loop(0, slots, turn, 0)
    link_own[...] = jnp.dot(link_state[...], link_self[...], preferred_element_type=jnp.float32)
    flow_own[...] = jnp.dot(flow_state[...], flow_self[...], preferred_element_type=jnp.float32)

    for h in range(HALVES):
        for way, (begin, _, near, _) in enumerate(ways):

            @pl.when(r == near)
            def _():
                gather1(h, (near - begin) % rows).wait_recv()
                relay1(h, way).start()

    for h in range(HALVES):
        for t in row_steps:
            unless(passed1(t), lambda: gather1(h, t).wait_recv())
        segment_sums(
            slots, link_keys, link_ends, link_blocks, lambda k, key: turned[k], flows[h], sums, link_parts, h
        )
        for t in col_steps:
            scatter2(h, t).start()

    totals = []
    for h in range(HALVES):
        total = link_parts[h, pl.ds(c * lb, lb)].astype(jnp.float32)
        for t in col_steps:
            scatter2(h, t).wait_recv()
            total = total + link_in[h, t].astype(jnp.float32)
        totals.append(total.reshape(lb * BS, W))
    fresh = updated(totals, link_state[...], link_own[...], link_gain, link_agg, link_out)
    link_next[...] = fresh
    for h in range(HALVES):
        for b in range(lb):
            links[h][c * lb + b] = fresh[b * BS : (b + 1) * BS, h * W : (h + 1) * W]
        for t in col_steps:
            if h > 0:
                gather3(h - 1, t).wait_send()
        for t in col_steps:
            gather3(h, t).start()

    for h in range(HALVES):
        for t in col_steps:
            gather3(h, t).wait_recv()
        segment_sums(
            slots, flow_keys, flow_ends, flow_blocks, lambda k, key: coefs[0, 0, key & 255], links[h], sums, flow_parts, h
        )
        for way, (begin, _, _, _) in enumerate(ways):
            pl.when(r == begin)(lambda: relay4(h, way).start())
        for t in row_steps:
            unless(ends_of(t) + joined4(t), lambda: scatter4(h, t).start())
    for h in range(HALVES):
        for way, (_, near, _, end) in enumerate(ways):

            @pl.when(r == near)
            def _():
                relay4(h, way).wait_recv()
                part = flow_parts[h, pl.ds(end * fb, fb)].astype(jnp.float32)
                part = part + relay_in[h, way].astype(jnp.float32)
                flow_parts[h, pl.ds(end * fb, fb)] = part.astype(jnp.bfloat16)
                scatter4(h, (end - near) % rows).start()

    totals = []
    for h in range(HALVES):
        total = flow_parts[h, pl.ds(r * fb, fb)].astype(jnp.float32)
        for t in row_steps:
            unless(met(t), lambda: scatter4(h, t).wait_recv())
            total = total + flow_in[h, t].astype(jnp.float32)
        totals.append(total.reshape(fb * BS, W))
    flow_next[...] = updated(totals, flow_state[...], flow_own[...], flow_gain, flow_agg, flow_out)

    for h in range(HALVES):
        for t in row_steps:
            if h == HALVES - 1:
                unless(ends_of(t), lambda: gather1(h, t).wait_send())
            unless(ends_of(t), lambda: scatter4(h, t).wait_send())
        for way, (begin, _, near, _) in enumerate(ways):
            pl.when(r == near)(lambda: relay1(h, way).wait_send())
            pl.when(r == begin)(lambda: relay4(h, way).wait_send())
        for t in col_steps:
            scatter2(h, t).wait_send()
            if h == HALVES - 1:
                gather3(h, t).wait_send()


def on_device(
    rows,
    cols,
    flow_state,
    link_state,
    incidence,
    tile_flow,
    tile_link,
    tile_live,
    link_gain,
    link_agg_weight,
    link_self_weight,
    link_out_weight,
    flow_gain,
    flow_agg_weight,
    flow_self_weight,
    flow_out_weight,
):
    slots = incidence.shape[2]
    fb, lb = flow_state.shape[0] // BS, link_state.shape[0] // BS
    flow_blocks, link_blocks = fb * rows, lb * cols
    vmem = pl.BlockSpec(memory_space=pltpu.VMEM)
    hbm = pl.BlockSpec(memory_space=pltpu.HBM)
    bf16, f32, i32 = jnp.bfloat16, jnp.float32, jnp.int32
    dma = pltpu.SemaphoreType.DMA
    return pl.pallas_call(
        functools.partial(kernel, rows, cols),
        out_shape=(
            jax.ShapeDtypeStruct(link_state.shape, bf16),
            jax.ShapeDtypeStruct(flow_state.shape, bf16),
        ),
        in_specs=[hbm] * 14,
        out_specs=(vmem, vmem),
        scratch_shapes=[
            pltpu.VMEM(flow_state.shape, bf16),
            pltpu.VMEM(link_state.shape, bf16),
            pltpu.VMEM(incidence.shape, bf16),
            *[pltpu.VMEM((H, H), bf16) for _ in range(6)],
            *[pltpu.VMEM((1, H), f32) for _ in range(2)],
            *[pltpu.SMEM((1, 1, slots), i32) for _ in range(3)],
            *[pltpu.VMEM((flow_blocks, BS, W), bf16) for _ in range(HALVES)],
            *[pltpu.VMEM((link_blocks, BS, W), bf16) for _ in range(HALVES)],
            pltpu.VMEM((HALVES, link_blocks, BS, W), bf16),
            pltpu.VMEM((HALVES, cols, lb, BS, W), bf16),
            pltpu.VMEM((HALVES, flow_blocks, BS, W), bf16),
            pltpu.VMEM((HALVES, rows, fb, BS, W), bf16),
            pltpu.VMEM((slots, BS, BS), bf16),
            pltpu.VMEM((slots, BS, W), f32),
            pltpu.VMEM((lb * BS, H), f32),
            pltpu.VMEM((fb * BS, H), f32),
            pltpu.SMEM((slots + 1,), i32),
            pltpu.SMEM((link_blocks,), i32),
            pltpu.SMEM((slots + 1,), i32),
            pltpu.SMEM((flow_blocks,), i32),
            dma((HALVES, rows)),
            dma((HALVES, rows)),
            dma((HALVES, cols)),
            dma((HALVES, cols)),
            dma((HALVES, cols)),
            dma((HALVES, cols)),
            dma((HALVES, rows)),
            dma((HALVES, rows)),
            dma((HALVES, fb)),
            dma((14,)),
            pltpu.VMEM((HALVES, 2, fb, BS, W), bf16),
            dma((HALVES, 2)),
            dma((HALVES, 2)),
            dma((HALVES, 2)),
        ],
        compiler_params=pltpu.CompilerParams(
            collective_id=0, has_side_effects=True, vmem_limit_bytes=60 * 1024 * 1024
        ),
        name="message_round",
    )(
        flow_state,
        link_state,
        incidence,
        link_agg_weight,
        link_self_weight,
        link_out_weight,
        flow_agg_weight,
        flow_self_weight,
        flow_out_weight,
        tile_flow,
        tile_link,
        tile_live,
        link_gain.reshape(1, H),
        flow_gain.reshape(1, H),
    )


def solution(mesh):
    return jax.shard_map(
        functools.partial(on_device, mesh.shape["row"], mesh.shape["col"]),
        mesh=mesh,
        in_specs=(
            P(("col", "row"), None),
            P(("row", "col"), None),
            P("row", "col", None, None, None),
            P("row", "col", None),
            P("row", "col", None),
            P("row", "col", None),
            P(),
            P(),
            P(),
            P(),
            P(),
            P(),
            P(),
            P(),
        ),
        out_specs=(P(("row", "col"), None), P(("col", "row"), None)),
        check_vma=False,
    )
```

```python
import functools

import jax
import jax.numpy as jnp
from jax import lax
from jax.experimental import pallas as pl
from jax.experimental.pallas import tpu as pltpu
from jax.sharding import PartitionSpec as P

H = 256
BS = 128
HALVES = 2
W = H // HALVES
MESH = pl.DeviceIdType.MESH


def sort_pairs(n):
    pairs = []
    p = 1
    while p < n:
        k = p
        while k >= 1:
            for j in range(k % p, n - k, 2 * k):
                for i in range(min(k, n - j - k)):
                    if (i + j) // (2 * p) == (i + j + k) // (2 * p):
                        pairs.append((i + j, i + j + k))
            k //= 2
        p *= 2
    return pairs


def order_slots(targets, sources, live, blocks, keys, ends):
    slots = targets.shape[2]
    held = []
    for s in range(slots):
        target = jnp.where(live[0, 0, s] == 1, targets[0, 0, s], blocks)
        held.append(target * 65536 + sources[0, 0, s] * 256 + s)
    for low, high in sort_pairs(slots):
        least, most = jnp.minimum(held[low], held[high]), jnp.maximum(held[low], held[high])
        held[low], held[high] = least, most
    keys[0] = jnp.int32(-1)
    for k in range(slots):
        keys[1 + k] = held[k]

    def count(b, carry):
        bound = (b + 1) * 65536
        below = jnp.int32(0)
        for k in range(slots):
            below = below + jnp.where(keys[1 + k] < bound, 1, 0)
        last = jnp.maximum(below - 1, 0)
        there = jnp.where(below > 0, jnp.where(lax.shift_right_logical(keys[1 + last], 16) == b, 1, 0), 0)
        ends[b] = last * 2 + there
        return carry

    lax.fori_loop(0, blocks, count, 0)


def segment_sums(slots, keys, ends, blocks, tile_of, source, sums, parts, half):
    unroll = 8 if slots % 8 == 0 else 1

    def steps(group, total):
        for inner in range(unroll):
            k = group * unroll + inner
            key = keys[1 + k]
            same = lax.shift_right_arithmetic(key, 16) == lax.shift_right_arithmetic(keys[k], 16)
            keep = jnp.where(same, 1.0, 0.0).astype(jnp.float32)
            piece = source[lax.shift_right_logical(key, 8) & 255]
            total = total * keep + jnp.dot(
                tile_of(k, key), piece, preferred_element_type=jnp.float32
            )
            sums[k] = total
        return total

    lax.fori_loop(0, slots // unroll, steps, jnp.zeros((BS, W), jnp.float32))

    def pick(b, carry):
        end = ends[b]
        there = jnp.where((end & 1) == 1, 1.0, 0.0).astype(jnp.float32)
        parts[half, b] = (sums[lax.shift_right_logical(end, 1)] * there).astype(jnp.bfloat16)
        return carry

    lax.fori_loop(0, blocks, pick, 0)


def gained(total, half, gain, agg_weight):
    cut = slice(half * W, (half + 1) * W)
    product = jnp.dot(
        (total * gain[:, cut]).astype(jnp.bfloat16), agg_weight[cut, :], preferred_element_type=jnp.float32
    )
    return jnp.sum(total * total, axis=-1, keepdims=True), product


def updated(square, product, state, own, out_weight):
    scale = lax.rsqrt(square * (1.0 / H) + 1e-05)
    before = own + product * scale
    hidden = (before / (1.0 + jnp.exp(-before))).astype(jnp.bfloat16)
    return (
        state.astype(jnp.float32) + jnp.dot(hidden, out_weight[...], preferred_element_type=jnp.float32)
    ).astype(jnp.bfloat16)


def kernel(
    rows,
    cols,
    flow_state_hbm,
    link_state_hbm,
    coefs_hbm,
    link_agg_hbm,
    link_self_hbm,
    link_out_hbm,
    flow_agg_hbm,
    flow_self_hbm,
    flow_out_hbm,
    tile_flow_hbm,
    tile_link_hbm,
    tile_live_hbm,
    link_gain_hbm,
    flow_gain_hbm,
    link_next,
    flow_next,
    flow_state,
    link_state,
    coefs,
    link_agg,
    link_self,
    link_out,
    flow_agg,
    flow_self,
    flow_out,
    link_gain,
    flow_gain,
    tile_flow,
    tile_link,
    tile_live,
    flows0,
    flows1,
    links0,
    links1,
    link_parts,
    link_in,
    flow_parts,
    flow_in,
    turned,
    sums,
    link_own,
    flow_own,
    link_keys,
    link_ends,
    flow_keys,
    flow_ends,
    send1,
    recv1,
    send2,
    recv2,
    send3,
    recv3,
    send4,
    recv4,
    own_sem,
    in_sem,
    relay_in,
    relay_send1,
    relay_send4,
    relay_recv4,
):
    flows, links = (flows0, flows1), (links0, links1)
    r, c = lax.axis_index("row"), lax.axis_index("col")
    slots = coefs.shape[2]
    fb, lb = flow_state.shape[0] // BS, link_state.shape[0] // BS
    flow_blocks, link_blocks = fb * rows, lb * cols

    def row_peer(t):
        return lax.rem(r + t, rows)

    def col_peer(t):
        return lax.rem(c + t, cols)

    def gather1(h, t):
        mine = flows[h].at[pl.ds(r * fb, fb)]
        return pltpu.make_async_remote_copy(
            src_ref=mine, dst_ref=mine, send_sem=send1.at[h, t], recv_sem=recv1.at[h, t],
            device_id=(row_peer(t), c), device_id_type=MESH,
        )

    def scatter2(h, t):
        peer = col_peer(t)
        return pltpu.make_async_remote_copy(
            src_ref=link_parts.at[h, pl.ds(peer * lb, lb)], dst_ref=link_in.at[h, t],
            send_sem=send2.at[h, t], recv_sem=recv2.at[h, t],
            device_id=(r, peer), device_id_type=MESH,
        )

    def gather3(h, t):
        mine = links[h].at[pl.ds(c * lb, lb)]
        return pltpu.make_async_remote_copy(
            src_ref=mine, dst_ref=mine, send_sem=send3.at[h, t], recv_sem=recv3.at[h, t],
            device_id=(r, col_peer(t)), device_id_type=MESH,
        )

    partner = c + 1 - 2 * lax.rem(c, 2)
    chip_steps = range(2, cols, 2)

    def relay3(h, t):
        shard = links[h].at[pl.ds(lax.rem(c + cols - t, cols) * lb, lb)]
        return pltpu.make_async_remote_copy(
            src_ref=shard, dst_ref=shard, send_sem=send3.at[h, t + 1], recv_sem=recv3.at[h, t + 1],
            device_id=(r, partner), device_id_type=MESH,
        )

    def scatter4(h, t):
        peer = row_peer(t)
        return pltpu.make_async_remote_copy(
            src_ref=flow_parts.at[h, pl.ds(peer * fb, fb)], dst_ref=flow_in.at[h, t],
            send_sem=send4.at[h, t], recv_sem=recv4.at[h, t],
            device_id=(peer, c), device_id_type=MESH,
        )

    last = rows - 1
    ways = ((0, 1, rows - 2, last), (last, last - 1, 1, 0)) if rows > 2 else ()

    def relay1(h, way):
        begin, _, near, end = ways[way]
        shard = flows[h].at[pl.ds(begin * fb, fb)]
        return pltpu.make_async_remote_copy(
            src_ref=shard, dst_ref=shard, send_sem=relay_send1.at[h, way],
            recv_sem=recv1.at[h, (end - begin) % rows],
            device_id=(end, c), device_id_type=MESH,
        )

    def relay4(h, way):
        begin, near, _, end = ways[way]
        return pltpu.make_async_remote_copy(
            src_ref=flow_parts.at[h, pl.ds(end * fb, fb)], dst_ref=relay_in.at[h, way],
            send_sem=relay_send4.at[h, way], recv_sem=relay_recv4.at[h, way],
            device_id=(near, c), device_id_type=MESH,
        )

    def unless(places, act):
        if not places:
            act()
            return
        free = r != places[0]
        for place in places[1:]:
            free = jnp.logical_and(free, r != place)
        pl.when(free)(act)

    def ends_of(t):
        return [begin for begin, _, _, end in ways if (end - begin) % rows == t]

    def met(t):
        return [end for begin, _, _, end in ways if (end - begin) % rows == t]

    def passed1(t):
        return [near for begin, _, near, _ in ways if (near - begin) % rows == t]

    def joined4(t):
        return [near for _, near, _, end in ways if (end - near) % rows == t]

    row_steps = sorted(range(1, rows), key=lambda t: (-min(t, rows - t), t))
    col_steps = range(1, cols)
    barrier = pltpu.get_barrier_semaphore()
    for t in row_steps:
        pl.semaphore_signal(barrier, inc=1, device_id=(row_peer(t), c), device_id_type=MESH)
    for t in col_steps:
        pl.semaphore_signal(barrier, inc=1, device_id=(r, col_peer(t)), device_id_type=MESH)
    own_in = [
        pltpu.make_async_copy(
            flow_state_hbm.at[pl.ds(b * BS, BS), pl.ds(h * W, W)], flows[h].at[r * fb + b], own_sem.at[h, b]
        )
        for h in range(HALVES)
        for b in range(fb)
    ]
    pairs = (
        (coefs_hbm, coefs),
        (link_state_hbm, link_state),
        (link_self_hbm, link_self),
        (flow_state_hbm, flow_state),
        (flow_self_hbm, flow_self),
        (link_agg_hbm, link_agg),
        (link_out_hbm, link_out),
        (flow_agg_hbm, flow_agg),
        (flow_out_hbm, flow_out),
        (link_gain_hbm, link_gain),
        (flow_gain_hbm, flow_gain),
    )
    tables = (
        (tile_flow_hbm, tile_flow),
        (tile_link_hbm, tile_link),
        (tile_live_hbm, tile_live),
    )
    tables_in = [pltpu.make_async_copy(a, b, in_sem.at[len(pairs) + n]) for n, (a, b) in enumerate(tables)]
    operands_in = [pltpu.make_async_copy(a, b, in_sem.at[n]) for n, (a, b) in enumerate(pairs)]
    for copy in own_in + tables_in + operands_in:
        copy.start()
    for copy in own_in:
        copy.wait()
    pl.semaphore_wait(barrier, rows + cols - 2)

    for h in range(HALVES):
        for t in row_steps:
            unless(ends_of(t), lambda: gather1(h, t).start())
    for h in range(HALVES):
        for way, (begin, _, _, end) in enumerate(ways):

            @pl.when(r == end)
            def _():
                flow_in[h, (end - begin) % rows] = jnp.zeros((fb, BS, W), jnp.bfloat16)

    for copy in tables_in:
        copy.wait()
    order_slots(tile_link, tile_flow, tile_live, link_blocks, link_keys, link_ends)
    order_slots(tile_flow, tile_link, tile_live, flow_blocks, flow_keys, flow_ends)

    for copy in operands_in:
        copy.wait()

    def pass_on(h):
        for way, (begin, _, near, _) in enumerate(ways):

            @pl.when(r == near)
            def _():
                gather1(h, (near - begin) % rows).wait_recv()
                relay1(h, way).start()

    pass_on(0)

    def turn(k, carry):
        turned[k] = coefs[0, 0, link_keys[1 + k] & 255].T
        return carry

    lax.fori_loop(0, slots, turn, 0)
    link_own[...] = jnp.dot(link_state[...], link_self[...], preferred_element_type=jnp.float32)
    flow_own[...] = jnp.dot(flow_state[...], flow_self[...], preferred_element_type=jnp.float32)

    pass_on(1)

    for h in range(HALVES):
        for t in row_steps:
            unless(passed1(t), lambda: gather1(h, t).wait_recv())
        segment_sums(
            slots, link_keys, link_ends, link_blocks, lambda k, key: turned[k], flows[h], sums, link_parts, h
        )
        for t in col_steps:
            scatter2(h, t).start()

    totals = []
    for h in range(HALVES):
        total = link_parts[h, pl.ds(c * lb, lb)].astype(jnp.float32)
        for t in col_steps:
            scatter2(h, t).wait_recv()
            total = total + link_in[h, t].astype(jnp.float32)
        square, product = gained(total.reshape(lb * BS, W), h, link_gain, link_agg)
        totals.append((square, product))
    square, product = (sum(terms[1:], terms[0]) for terms in zip(*totals))
    fresh = updated(square, product, link_state[...], link_own[...], link_out)
    for h in range(HALVES):
        for b in range(lb):
            links[h][c * lb + b] = fresh[b * BS : (b + 1) * BS, h * W : (h + 1) * W]
        for t in chip_steps:
            gather3(h, t).start()
        relay3(h, 0).start()
    link_next[...] = fresh

    for h in range(HALVES):
        for t in chip_steps:
            gather3(h, t).wait_recv()
            relay3(h, t).start()
        for t in (0, *chip_steps):
            relay3(h, t).wait_recv()
        segment_sums(
            slots, flow_keys, flow_ends, flow_blocks, lambda k, key: coefs[0, 0, key & 255], links[h], sums, flow_parts, h
        )
        for way, (begin, _, _, _) in enumerate(ways):
            pl.when(r == begin)(lambda: relay4(h, way).start())
        for t in row_steps:
            unless(ends_of(t) + joined4(t), lambda: scatter4(h, t).start())
    for h in range(HALVES):
        for way, (_, near, _, end) in enumerate(ways):

            @pl.when(r == near)
            def _():
                relay4(h, way).wait_recv()
                part = flow_parts[h, pl.ds(end * fb, fb)].astype(jnp.float32)
                part = part + relay_in[h, way].astype(jnp.float32)
                flow_parts[h, pl.ds(end * fb, fb)] = part.astype(jnp.bfloat16)
                scatter4(h, (end - near) % rows).start()

    totals = []
    for h in range(HALVES):
        total = flow_parts[h, pl.ds(r * fb, fb)].astype(jnp.float32)
        for t in row_steps:
            unless(met(t), lambda: scatter4(h, t).wait_recv())
            total = total + flow_in[h, t].astype(jnp.float32)
        square, product = gained(total.reshape(fb * BS, W), h, flow_gain, flow_agg)
        totals.append((square, product))
    square, product = (sum(terms[1:], terms[0]) for terms in zip(*totals))
    flow_next[...] = updated(square, product, flow_state[...], flow_own[...], flow_out)

    for h in range(HALVES):
        for t in row_steps:
            unless(ends_of(t), lambda: gather1(h, t).wait_send())
            unless(ends_of(t), lambda: scatter4(h, t).wait_send())
        for way, (begin, _, near, _) in enumerate(ways):
            pl.when(r == near)(lambda: relay1(h, way).wait_send())
            pl.when(r == begin)(lambda: relay4(h, way).wait_send())
        for t in col_steps:
            scatter2(h, t).wait_send()
        for t in chip_steps:
            gather3(h, t).wait_send()
        for t in (0, *chip_steps):
            relay3(h, t).wait_send()


def on_device(
    rows,
    cols,
    flow_state,
    link_state,
    incidence,
    tile_flow,
    tile_link,
    tile_live,
    link_gain,
    link_agg_weight,
    link_self_weight,
    link_out_weight,
    flow_gain,
    flow_agg_weight,
    flow_self_weight,
    flow_out_weight,
):
    slots = incidence.shape[2]
    fb, lb = flow_state.shape[0] // BS, link_state.shape[0] // BS
    flow_blocks, link_blocks = fb * rows, lb * cols
    vmem = pl.BlockSpec(memory_space=pltpu.VMEM)
    hbm = pl.BlockSpec(memory_space=pltpu.HBM)
    bf16, f32, i32 = jnp.bfloat16, jnp.float32, jnp.int32
    dma = pltpu.SemaphoreType.DMA
    return pl.pallas_call(
        functools.partial(kernel, rows, cols),
        out_shape=(
            jax.ShapeDtypeStruct(link_state.shape, bf16),
            jax.ShapeDtypeStruct(flow_state.shape, bf16),
        ),
        in_specs=[hbm] * 14,
        out_specs=(vmem, vmem),
        scratch_shapes=[
            pltpu.VMEM(flow_state.shape, bf16),
            pltpu.VMEM(link_state.shape, bf16),
            pltpu.VMEM(incidence.shape, bf16),
            *[pltpu.VMEM((H, H), bf16) for _ in range(6)],
            *[pltpu.VMEM((1, H), f32) for _ in range(2)],
            *[pltpu.SMEM((1, 1, slots), i32) for _ in range(3)],
            *[pltpu.VMEM((flow_blocks, BS, W), bf16) for _ in range(HALVES)],
            *[pltpu.VMEM((link_blocks, BS, W), bf16) for _ in range(HALVES)],
            pltpu.VMEM((HALVES, link_blocks, BS, W), bf16),
            pltpu.VMEM((HALVES, cols, lb, BS, W), bf16),
            pltpu.VMEM((HALVES, flow_blocks, BS, W), bf16),
            pltpu.VMEM((HALVES, rows, fb, BS, W), bf16),
            pltpu.VMEM((slots, BS, BS), bf16),
            pltpu.VMEM((slots, BS, W), f32),
            pltpu.VMEM((lb * BS, H), f32),
            pltpu.VMEM((fb * BS, H), f32),
            pltpu.SMEM((slots + 1,), i32),
            pltpu.SMEM((link_blocks,), i32),
            pltpu.SMEM((slots + 1,), i32),
            pltpu.SMEM((flow_blocks,), i32),
            dma((HALVES, rows)),
            dma((HALVES, rows)),
            dma((HALVES, cols)),
            dma((HALVES, cols)),
            dma((HALVES, cols)),
            dma((HALVES, cols)),
            dma((HALVES, rows)),
            dma((HALVES, rows)),
            dma((HALVES, fb)),
            dma((14,)),
            pltpu.VMEM((HALVES, 2, fb, BS, W), bf16),
            dma((HALVES, 2)),
            dma((HALVES, 2)),
            dma((HALVES, 2)),
        ],
        compiler_params=pltpu.CompilerParams(
            collective_id=0, has_side_effects=True, vmem_limit_bytes=60 * 1024 * 1024
        ),
        name="message_round",
    )(
        flow_state,
        link_state,
        incidence,
        link_agg_weight,
        link_self_weight,
        link_out_weight,
        flow_agg_weight,
        flow_self_weight,
        flow_out_weight,
        tile_flow,
        tile_link,
        tile_live,
        link_gain.reshape(1, H),
        flow_gain.reshape(1, H),
    )


def solution(mesh):
    return jax.shard_map(
        functools.partial(on_device, mesh.shape["row"], mesh.shape["col"]),
        mesh=mesh,
        in_specs=(
            P(("col", "row"), None),
            P(("row", "col"), None),
            P("row", "col", None, None, None),
            P("row", "col", None),
            P("row", "col", None),
            P("row", "col", None),
            P(),
            P(),
            P(),
            P(),
            P(),
            P(),
            P(),
            P(),
        ),
        out_specs=(P(("row", "col"), None), P(("col", "row"), None)),
        check_vma=False,
    )
```

```python
import functools

import jax
import jax.numpy as jnp
from jax import lax
from jax.experimental import pallas as pl
from jax.experimental.pallas import tpu as pltpu
from jax.sharding import PartitionSpec as P

H = 256
BS = 128
HALVES = 2
W = H // HALVES
MESH = pl.DeviceIdType.MESH


def sort_pairs(n):
    pairs = []
    p = 1
    while p < n:
        k = p
        while k >= 1:
            for j in range(k % p, n - k, 2 * k):
                for i in range(min(k, n - j - k)):
                    if (i + j) // (2 * p) == (i + j + k) // (2 * p):
                        pairs.append((i + j, i + j + k))
            k //= 2
        p *= 2
    return pairs


def order_slots(targets, sources, live, blocks, keys, ends):
    slots = targets.shape[2]
    held = []
    for s in range(slots):
        target = jnp.where(live[0, 0, s] == 1, targets[0, 0, s], blocks)
        held.append(target * 65536 + sources[0, 0, s] * 256 + s)
    for low, high in sort_pairs(slots):
        least, most = jnp.minimum(held[low], held[high]), jnp.maximum(held[low], held[high])
        held[low], held[high] = least, most
    keys[0] = jnp.int32(-1)
    for k in range(slots):
        keys[1 + k] = held[k]

    def count(b, carry):
        bound = (b + 1) * 65536
        below = jnp.int32(0)
        for k in range(slots):
            below = below + jnp.where(keys[1 + k] < bound, 1, 0)
        last = jnp.maximum(below - 1, 0)
        there = jnp.where(below > 0, jnp.where(lax.shift_right_logical(keys[1 + last], 16) == b, 1, 0), 0)
        ends[b] = last * 2 + there
        return carry

    lax.fori_loop(0, blocks, count, 0)


def segment_sums(slots, keys, ends, blocks, tile_of, source, sums, parts, half):
    unroll = 8 if slots % 8 == 0 else 1

    def steps(group, total):
        for inner in range(unroll):
            k = group * unroll + inner
            key = keys[1 + k]
            same = lax.shift_right_arithmetic(key, 16) == lax.shift_right_arithmetic(keys[k], 16)
            keep = jnp.where(same, 1.0, 0.0).astype(jnp.float32)
            piece = source[lax.shift_right_logical(key, 8) & 255]
            total = total * keep + jnp.dot(
                tile_of(k, key), piece, preferred_element_type=jnp.float32
            )
            sums[k] = total
        return total

    lax.fori_loop(0, slots // unroll, steps, jnp.zeros((BS, W), jnp.float32))

    def pick(b, carry):
        end = ends[b]
        there = jnp.where((end & 1) == 1, 1.0, 0.0).astype(jnp.float32)
        parts[half, b] = (sums[lax.shift_right_logical(end, 1)] * there).astype(jnp.bfloat16)
        return carry

    lax.fori_loop(0, blocks, pick, 0)


def gained(total, half, gain, agg_weight):
    cut = slice(half * W, (half + 1) * W)
    product = jnp.dot(
        (total * gain[:, cut]).astype(jnp.bfloat16), agg_weight[cut, :], preferred_element_type=jnp.float32
    )
    return jnp.sum(total * total, axis=-1, keepdims=True), product


def updated(square, product, state, own, out_weight):
    scale = lax.rsqrt(square * (1.0 / H) + 1e-05)
    before = own + product * scale
    hidden = (before / (1.0 + jnp.exp(-before))).astype(jnp.bfloat16)
    return (
        state.astype(jnp.float32) + jnp.dot(hidden, out_weight[...], preferred_element_type=jnp.float32)
    ).astype(jnp.bfloat16)


def kernel(
    rows,
    cols,
    flow_state_hbm,
    link_state_hbm,
    coefs_hbm,
    link_agg_hbm,
    link_self_hbm,
    link_out_hbm,
    flow_agg_hbm,
    flow_self_hbm,
    flow_out_hbm,
    tile_flow_hbm,
    tile_link_hbm,
    tile_live_hbm,
    link_gain_hbm,
    flow_gain_hbm,
    link_next,
    flow_next,
    flow_state,
    link_state,
    coefs,
    link_agg,
    link_self,
    link_out,
    flow_agg,
    flow_self,
    flow_out,
    link_gain,
    flow_gain,
    tile_flow,
    tile_link,
    tile_live,
    flows0,
    flows1,
    links0,
    links1,
    link_parts,
    link_in,
    flow_parts,
    flow_in,
    turned,
    sums,
    link_own,
    flow_own,
    link_keys,
    link_ends,
    flow_keys,
    flow_ends,
    send1,
    recv1,
    send2,
    recv2,
    send3,
    recv3,
    send4,
    recv4,
    own_sem,
    in_sem,
    relay_in,
    relay_send1,
    relay_send4,
    relay_recv4,
):
    flows, links = (flows0, flows1), (links0, links1)
    r, c = lax.axis_index("row"), lax.axis_index("col")
    slots = coefs.shape[2]
    fb, lb = flow_state.shape[0] // BS, link_state.shape[0] // BS
    flow_blocks, link_blocks = fb * rows, lb * cols

    def row_peer(t):
        return lax.rem(r + t, rows)

    def col_peer(t):
        return lax.rem(c + t, cols)

    def gather1(h, t):
        mine = flows[h].at[pl.ds(r * fb, fb)]
        return pltpu.make_async_remote_copy(
            src_ref=mine, dst_ref=mine, send_sem=send1.at[h, t], recv_sem=recv1.at[h, t],
            device_id=(row_peer(t), c), device_id_type=MESH,
        )

    def scatter2(h, t):
        peer = col_peer(t)
        return pltpu.make_async_remote_copy(
            src_ref=link_parts.at[h, pl.ds(peer * lb, lb)], dst_ref=link_in.at[h, t],
            send_sem=send2.at[h, t], recv_sem=recv2.at[h, t],
            device_id=(r, peer), device_id_type=MESH,
        )

    def gather3(h, t):
        mine = links[h].at[pl.ds(c * lb, lb)]
        return pltpu.make_async_remote_copy(
            src_ref=mine, dst_ref=mine, send_sem=send3.at[h, t], recv_sem=recv3.at[h, t],
            device_id=(r, col_peer(t)), device_id_type=MESH,
        )

    partner = c + 1 - 2 * lax.rem(c, 2)
    chip_steps = range(2, cols, 2)

    def relay3(h, t):
        shard = links[h].at[pl.ds(lax.rem(c + cols - t, cols) * lb, lb)]
        return pltpu.make_async_remote_copy(
            src_ref=shard, dst_ref=shard, send_sem=send3.at[h, t + 1], recv_sem=recv3.at[h, t + 1],
            device_id=(r, partner), device_id_type=MESH,
        )

    def scatter4(h, t):
        peer = row_peer(t)
        return pltpu.make_async_remote_copy(
            src_ref=flow_parts.at[h, pl.ds(peer * fb, fb)], dst_ref=flow_in.at[h, t],
            send_sem=send4.at[h, t], recv_sem=recv4.at[h, t],
            device_id=(peer, c), device_id_type=MESH,
        )

    last = rows - 1
    ways = ((0, 1, rows - 2, last), (last, last - 1, 1, 0)) if rows > 2 else ()

    def relay1(h, way):
        begin, _, near, end = ways[way]
        shard = flows[h].at[pl.ds(begin * fb, fb)]
        return pltpu.make_async_remote_copy(
            src_ref=shard, dst_ref=shard, send_sem=relay_send1.at[h, way],
            recv_sem=recv1.at[h, (end - begin) % rows],
            device_id=(end, c), device_id_type=MESH,
        )

    def relay4(h, way):
        begin, near, _, end = ways[way]
        return pltpu.make_async_remote_copy(
            src_ref=flow_parts.at[h, pl.ds(end * fb, fb)], dst_ref=relay_in.at[h, way],
            send_sem=relay_send4.at[h, way], recv_sem=relay_recv4.at[h, way],
            device_id=(near, c), device_id_type=MESH,
        )

    def unless(places, act):
        if not places:
            act()
            return
        free = r != places[0]
        for place in places[1:]:
            free = jnp.logical_and(free, r != place)
        pl.when(free)(act)

    def ends_of(t):
        return [begin for begin, _, _, end in ways if (end - begin) % rows == t]

    def met(t):
        return [end for begin, _, _, end in ways if (end - begin) % rows == t]

    def passed1(t):
        return [near for begin, _, near, _ in ways if (near - begin) % rows == t]

    def joined4(t):
        return [near for _, near, _, end in ways if (end - near) % rows == t]

    row_steps = sorted(range(1, rows), key=lambda t: (-min(t, rows - t), t))
    col_steps = range(1, cols)
    barrier = pltpu.get_barrier_semaphore()
    for t in row_steps:
        pl.semaphore_signal(barrier, inc=1, device_id=(row_peer(t), c), device_id_type=MESH)
    for t in col_steps:
        pl.semaphore_signal(barrier, inc=1, device_id=(r, col_peer(t)), device_id_type=MESH)
    own_in = [
        pltpu.make_async_copy(
            flow_state_hbm.at[pl.ds(b * BS, BS), pl.ds(h * W, W)], flows[h].at[r * fb + b], own_sem.at[h, b]
        )
        for h in range(HALVES)
        for b in range(fb)
    ]
    pairs = (
        (coefs_hbm, coefs),
        (link_state_hbm, link_state),
        (link_self_hbm, link_self),
        (flow_state_hbm, flow_state),
        (flow_self_hbm, flow_self),
        (link_agg_hbm, link_agg),
        (link_out_hbm, link_out),
        (flow_agg_hbm, flow_agg),
        (flow_out_hbm, flow_out),
        (link_gain_hbm, link_gain),
        (flow_gain_hbm, flow_gain),
    )
    tables = (
        (tile_flow_hbm, tile_flow),
        (tile_link_hbm, tile_link),
        (tile_live_hbm, tile_live),
    )
    tables_in = [pltpu.make_async_copy(a, b, in_sem.at[len(pairs) + n]) for n, (a, b) in enumerate(tables)]
    operands_in = [pltpu.make_async_copy(a, b, in_sem.at[n]) for n, (a, b) in enumerate(pairs)]
    for copy in own_in + tables_in + operands_in:
        copy.start()
    for copy in own_in:
        copy.wait()
    pl.semaphore_wait(barrier, rows + cols - 2)

    for h in range(HALVES):
        for t in row_steps:
            unless(ends_of(t), lambda: gather1(h, t).start())
    for h in range(HALVES):
        for way, (begin, _, _, end) in enumerate(ways):

            @pl.when(r == end)
            def _():
                flow_in[h, (end - begin) % rows] = jnp.zeros((fb, BS, W), jnp.bfloat16)

    for copy in tables_in:
        copy.wait()
    order_slots(tile_link, tile_flow, tile_live, link_blocks, link_keys, link_ends)
    order_slots(tile_flow, tile_link, tile_live, flow_blocks, flow_keys, flow_ends)

    for copy in operands_in:
        copy.wait()

    def pass_on(h):
        for way, (begin, _, near, _) in enumerate(ways):

            @pl.when(r == near)
            def _():
                gather1(h, (near - begin) % rows).wait_recv()
                relay1(h, way).start()

    pass_on(0)

    def turn(k, carry):
        turned[k] = coefs[0, 0, link_keys[1 + k] & 255].T
        return carry

    lax.fori_loop(0, slots, turn, 0)
    link_own[...] = jnp.dot(link_state[...], link_self[...], preferred_element_type=jnp.float32)
    flow_own[...] = jnp.dot(flow_state[...], flow_self[...], preferred_element_type=jnp.float32)

    pass_on(1)

    for h in range(HALVES):
        for t in row_steps:
            unless(passed1(t), lambda: gather1(h, t).wait_recv())
        segment_sums(
            slots, link_keys, link_ends, link_blocks, lambda k, key: turned[k], flows[h], sums, link_parts, h
        )
        for t in col_steps:
            scatter2(h, t).start()

    totals = []
    for h in range(HALVES):
        total = link_parts[h, pl.ds(c * lb, lb)].astype(jnp.float32)
        for t in col_steps:
            scatter2(h, t).wait_recv()
            total = total + link_in[h, t].astype(jnp.float32)
        square, product = gained(total.reshape(lb * BS, W), h, link_gain, link_agg)
        totals.append((square, product))
    square, product = (sum(terms[1:], terms[0]) for terms in zip(*totals))
    fresh = updated(square, product, link_state[...], link_own[...], link_out)
    for h in range(HALVES):
        for b in range(lb):
            links[h][c * lb + b] = fresh[b * BS : (b + 1) * BS, h * W : (h + 1) * W]
        for t in chip_steps:
            gather3(h, t).start()
        relay3(h, 0).start()
    link_next[...] = fresh

    for h in range(HALVES):
        for t in chip_steps:
            gather3(h, t).wait_recv()
            relay3(h, t).start()
        for t in (0, *chip_steps):
            relay3(h, t).wait_recv()
        segment_sums(
            slots, flow_keys, flow_ends, flow_blocks, lambda k, key: coefs[0, 0, key & 255], links[h], sums, flow_parts, h
        )
        for way, (begin, _, _, _) in enumerate(ways):
            pl.when(r == begin)(lambda: relay4(h, way).start())
        for t in row_steps:
            unless(ends_of(t) + joined4(t), lambda: scatter4(h, t).start())
    for h in range(HALVES):
        for way, (_, near, _, end) in enumerate(ways):

            @pl.when(r == near)
            def _():
                relay4(h, way).wait_recv()
                part = flow_parts[h, pl.ds(end * fb, fb)].astype(jnp.float32)
                part = part + relay_in[h, way].astype(jnp.float32)
                flow_parts[h, pl.ds(end * fb, fb)] = part.astype(jnp.bfloat16)
                scatter4(h, (end - near) % rows).start()

    totals = []
    for h in range(HALVES):
        total = flow_parts[h, pl.ds(r * fb, fb)].astype(jnp.float32)
        for t in row_steps:
            unless(met(t), lambda: scatter4(h, t).wait_recv())
            total = total + flow_in[h, t].astype(jnp.float32)
        square, product = gained(total.reshape(fb * BS, W), h, flow_gain, flow_agg)
        totals.append((square, product))
    square, product = (sum(terms[1:], terms[0]) for terms in zip(*totals))
    flow_next[...] = updated(square, product, flow_state[...], flow_own[...], flow_out)

    for h in range(HALVES):
        for t in row_steps:
            unless(ends_of(t), lambda: gather1(h, t).wait_send())
            unless(ends_of(t), lambda: scatter4(h, t).wait_send())
        for way, (begin, _, near, _) in enumerate(ways):
            pl.when(r == near)(lambda: relay1(h, way).wait_send())
            pl.when(r == begin)(lambda: relay4(h, way).wait_send())
        for t in col_steps:
            scatter2(h, t).wait_send()
        for t in chip_steps:
            gather3(h, t).wait_send()
        for t in (0, *chip_steps):
            relay3(h, t).wait_send()


def on_device(
    rows,
    cols,
    flow_state,
    link_state,
    incidence,
    tile_flow,
    tile_link,
    tile_live,
    link_gain,
    link_agg_weight,
    link_self_weight,
    link_out_weight,
    flow_gain,
    flow_agg_weight,
    flow_self_weight,
    flow_out_weight,
):
    slots = incidence.shape[2]
    fb, lb = flow_state.shape[0] // BS, link_state.shape[0] // BS
    flow_blocks, link_blocks = fb * rows, lb * cols
    vmem = pl.BlockSpec(memory_space=pltpu.VMEM)
    hbm = pl.BlockSpec(memory_space=pltpu.HBM)
    bf16, f32, i32 = jnp.bfloat16, jnp.float32, jnp.int32
    dma = pltpu.SemaphoreType.DMA
    return pl.pallas_call(
        functools.partial(kernel, rows, cols),
        out_shape=(
            pltpu.VMEM(link_state.shape, bf16),
            pltpu.VMEM(flow_state.shape, bf16),
        ),
        in_specs=[hbm] * 14,
        out_specs=(vmem, vmem),
        scratch_shapes=[
            pltpu.VMEM(flow_state.shape, bf16),
            pltpu.VMEM(link_state.shape, bf16),
            pltpu.VMEM(incidence.shape, bf16),
            *[pltpu.VMEM((H, H), bf16) for _ in range(6)],
            *[pltpu.VMEM((1, H), f32) for _ in range(2)],
            *[pltpu.SMEM((1, 1, slots), i32) for _ in range(3)],
            *[pltpu.VMEM((flow_blocks, BS, W), bf16) for _ in range(HALVES)],
            *[pltpu.VMEM((link_blocks, BS, W), bf16) for _ in range(HALVES)],
            pltpu.VMEM((HALVES, link_blocks, BS, W), bf16),
            pltpu.VMEM((HALVES, cols, lb, BS, W), bf16),
            pltpu.VMEM((HALVES, flow_blocks, BS, W), bf16),
            pltpu.VMEM((HALVES, rows, fb, BS, W), bf16),
            pltpu.VMEM((slots, BS, BS), bf16),
            pltpu.VMEM((slots, BS, W), f32),
            pltpu.VMEM((lb * BS, H), f32),
            pltpu.VMEM((fb * BS, H), f32),
            pltpu.SMEM((slots + 1,), i32),
            pltpu.SMEM((link_blocks,), i32),
            pltpu.SMEM((slots + 1,), i32),
            pltpu.SMEM((flow_blocks,), i32),
            dma((HALVES, rows)),
            dma((HALVES, rows)),
            dma((HALVES, cols)),
            dma((HALVES, cols)),
            dma((HALVES, cols)),
            dma((HALVES, cols)),
            dma((HALVES, rows)),
            dma((HALVES, rows)),
            dma((HALVES, fb)),
            dma((14,)),
            pltpu.VMEM((HALVES, 2, fb, BS, W), bf16),
            dma((HALVES, 2)),
            dma((HALVES, 2)),
            dma((HALVES, 2)),
        ],
        compiler_params=pltpu.CompilerParams(
            collective_id=0, has_side_effects=True, vmem_limit_bytes=60 * 1024 * 1024
        ),
        name="message_round",
    )(
        flow_state,
        link_state,
        incidence,
        link_agg_weight,
        link_self_weight,
        link_out_weight,
        flow_agg_weight,
        flow_self_weight,
        flow_out_weight,
        tile_flow,
        tile_link,
        tile_live,
        link_gain.reshape(1, H),
        flow_gain.reshape(1, H),
    )


def solution(mesh):
    return jax.shard_map(
        functools.partial(on_device, mesh.shape["row"], mesh.shape["col"]),
        mesh=mesh,
        in_specs=(
            P(("col", "row"), None),
            P(("row", "col"), None),
            P("row", "col", None, None, None),
            P("row", "col", None),
            P("row", "col", None),
            P("row", "col", None),
            P(),
            P(),
            P(),
            P(),
            P(),
            P(),
            P(),
            P(),
        ),
        out_specs=(P(("row", "col"), None), P(("col", "row"), None)),
        check_vma=False,
    )
```
